512 devices in a mesh: tm: 32 (over x, y, core), panel: 16 (over z).
Axes of the slice: x: 4, y: 4, z: 16, core: 2. Of those that a mesh axis runs over, the one named last changes fastest.
Arguments:
- elem_trans: float32 [32, 1024, 1024], P('tm', 'panel'), may hold values from -0.1875 to 0.1875
- elem_cov: float32 [32, 1024, 1024], P('tm', 'panel'), may hold values from -1 to 12, as said below
- elem_info: float32 [32, 1024, 1024], P('tm', 'panel'), may hold values from -1 to 8, as said below
- elem_mean: float32 [32, 1024], P('tm', 'panel'), may hold values from -6 to 6
- elem_infovec: float32 [32, 1024], P('tm', 'panel'), may hold values from -6 to 6
Outputs:
- new_cov: float32 [32, 1024, 1024], P('tm', 'panel')
- new_mean: float32 [32, 1024], P('tm', 'panel')
The draws below stay inside these ranges and needn't reach their ends.
Inputs may be any that keep to these rules, and one draw needn't show every extreme that they name: `elem_cov`: each group's matrix is symmetric positive definite. `elem_info`: each group's matrix is symmetric positive definite.
All inputs are finite; a program needn't handle non-finite values.
Results may differ from the reference program's by a relative error of at most 0.000064.
Values sent between devices are 32-bit elements; how exact they have to be, the bound alone decides.
A program may use at most 128 MiB of HBM per device.

```python
import math
import jax
import jax.numpy as jnp
from jax import lax

N = 1024
GROUPS = 32
HALF = 16


def symmetric_draw(key, diag_low, diag_high, spread):
    key_diag, key_off = jax.random.split(key)
    diagonal = jnp.exp(jax.random.uniform(key_diag, (GROUPS, N), jnp.float32, math.log(diag_low), math.log(diag_high)))
    limit = spread * 0.735 / math.sqrt(N)
    offdiag = jax.random.uniform(key_off, (GROUPS, N, N), jnp.float32, -limit, limit)
    offdiag = 0.5 * (offdiag + jnp.swapaxes(offdiag, 1, 2))
    identity_mask = jnp.eye(N, dtype=jnp.float32)
    return offdiag * (1.0 - identity_mask) + diagonal[:, :, None] * identity_mask


def draw_elem_cov(key, part):
    key = jax.random.fold_in(key, 11)
    return symmetric_draw(key, 1.0, 4.0, 1.0)


def draw_elem_info(key, part):
    key = jax.random.fold_in(key, 23)
    return symmetric_draw(key, 1.0, 3.0, 0.8)


def shard_levels(own_key, shape, cuts, least, top_value):
    loudness = 1.0
    for position, shards_of in cuts:
        heights = jax.random.uniform(jax.random.fold_in(jax.random.fold_in(own_key, 6), position), (shards_of,), jnp.float32, least / len(cuts), top_value / len(cuts))
        loudness = loudness * jnp.repeat(jnp.exp(heights), shape[position] // shards_of).reshape((-1,) + (1,) * (len(shape) - 1 - position))
    return loudness


def normal_values(own_key, extent, scale, reach, pieces=(), held_as=jnp.bfloat16):
    result = scale * jax.random.normal(own_key, extent, jnp.float32)
    if pieces:
        result = result * shard_levels(own_key, extent, pieces, -0.22, 0.18)
    return jnp.clip(result, -reach, reach).astype(held_as)


def setup_inputs(seed: int = 0) -> dict:
    key_list = jax.random.split(jax.random.key(seed), 6)
    elem_trans = normal_values(key_list[0], (GROUPS, N, N), N ** -0.5, 0.1875, ((0, 32), (1, 16)), jnp.float32)
    elem_cov = draw_elem_cov(jax.random.fold_in(key_list[5], 71), 0)
    elem_info = draw_elem_info(jax.random.fold_in(key_list[5], 71), 0)
    elem_mean = normal_values(key_list[3], (GROUPS, N), 1.0, 6.0, ((0, 32), (1, 16)), jnp.float32)
    elem_infovec = normal_values(key_list[4], (GROUPS, N), 1.0, 6.0, ((0, 32), (1, 16)), jnp.float32)
    return dict(elem_trans=elem_trans, elem_cov=elem_cov, elem_info=elem_info, elem_mean=elem_mean, elem_infovec=elem_infovec)


HIGHEST = lax.Precision.HIGHEST

def combine_pair(operands):
    prev_cov, prev_mean, transition, covariance, information, state_mean, info_vector = operands
    identity_matrix = jnp.eye(N, dtype=jnp.float32)
    lower_factor = jnp.linalg.cholesky(prev_cov)
    coupling = jnp.dot(information, lower_factor, precision=HIGHEST)
    inner = identity_matrix + jnp.dot(lower_factor.T, coupling, precision=HIGHEST)
    inner_factor = jnp.linalg.cholesky(inner)
    mixed = jnp.dot(transition, lower_factor, precision=HIGHEST)
    factor = jax.scipy.linalg.solve_triangular(inner_factor, mixed.T, lower=True).T
    combined_cov = jnp.dot(factor, factor.T, precision=HIGHEST) + covariance
    right_side = jax.scipy.linalg.solve_triangular(lower_factor, prev_mean, lower=True)
    right_side = right_side + jnp.dot(info_vector, lower_factor, precision=HIGHEST)
    weight = jax.scipy.linalg.cho_solve((inner_factor, True), right_side)
    combined_mean = jnp.dot(mixed, weight, precision=HIGHEST) + state_mean
    return (combined_cov, combined_mean)

def reference(elem_trans, elem_cov, elem_info, elem_mean, elem_infovec):
    upper_cov, upper_mean = lax.map(combine_pair, (elem_cov[:HALF], elem_mean[:HALF], elem_trans[HALF:], elem_cov[HALF:], elem_info[HALF:], elem_mean[HALF:], elem_infovec[HALF:]))
    new_cov = jnp.concatenate([elem_cov[:HALF], upper_cov], axis=0)
    new_mean = jnp.concatenate([elem_mean[:HALF], upper_mean], axis=0)
    return (new_cov, new_mean)
```

```python
import functools

import jax
import jax.numpy as jnp
from jax import lax
from jax.experimental import pallas as pl
from jax.experimental.pallas import tpu as pltpu
from jax.sharding import PartitionSpec as P

MESH = pl.DeviceIdType.MESH
HIGHEST = lax.Precision.HIGHEST
F32 = jnp.float32
BF16 = jnp.bfloat16
ROWS = 64
HALF = 32
LANES = 128
LAG = 3
TOLERANCE = 1e-5


def split(value):
    high = value.astype(BF16)
    return high, (value - high.astype(F32)).astype(BF16)


def dot(left, right):
    return jnp.dot(left, right, preferred_element_type=F32)


def dot_nt(left, right):
    return lax.dot_general(left, right, (((1,), (1,)), ((), ())), preferred_element_type=F32)


def place(T):
    t = lax.axis_index("tm")
    z = lax.axis_index("panel")
    distance = T // 2
    core = lax.rem(t, 2)
    low = t < distance
    base_low = lax.rem(t, distance) - core
    base_high = base_low + distance
    return t, z, core, low, base_low, base_high


def await_bytes(ref, sem):
    pltpu.make_async_copy(ref, ref, sem).wait()


def solve_kernel(
    T, Z,
    trans, cov, info, mean, infovec,
    rows_out, small_out, pj_out, a_out, v_out,
    pj, av, vv, st_pj, st_v, p_high, p_low, j_high, j_low, series, scale,
    recv, send, shift_recv, shift_send, out_sem,
):
    t, z, core, low, base_low, base_high = place(T)
    supers = Z // 2
    near = supers // 2
    H = Z // 2
    size = Z * ROWS
    partner = t + 1 - 2 * core
    opposite = jnp.where(low, base_high, base_low)
    up, down = lax.rem(z + 1, Z), lax.rem(z + Z - 1, Z)

    barrier = pltpu.get_barrier_semaphore()
    for device in ((t, up), (t, down), (partner, z), (opposite, z), (opposite + 1, z)):
        pl.semaphore_signal(barrier, inc=1, device_id=device, device_id_type=MESH)

    own_super = z // 2
    for k in range(near + 1):
        column = pl.multiple_of(lax.rem(own_super + k, supers) * LANES, LANES)
        block = jnp.where(low, cov[:, pl.ds(column, LANES)], info[:, pl.ds(column, LANES)])
        st_pj[0, k] = block[:HALF]
        st_pj[1, k] = block[HALF:]
    vector = jnp.where(low, mean[...], infovec[...])
    nothing = jnp.zeros_like(vector)
    vector = jnp.where(
        lax.rem(z, 2) == 0,
        jnp.concatenate([vector, nothing], axis=1),
        jnp.concatenate([nothing, vector], axis=1),
    )
    lane = lax.broadcasted_iota(jnp.int32, (8, LANES), 1)
    for h in range(2):
        start = lax.rem(z, 2) * ROWS + h * HALF
        mine = jnp.logical_and(lane >= start, lane < start + HALF)
        st_v[h] = jnp.where(mine, jnp.broadcast_to(vector, (8, LANES)), 0.0)
    pl.semaphore_wait(barrier, 5)

    target_base = jnp.where(core == 0, base_low, base_high)
    high = jnp.logical_not(low)
    low_has_far = own_super < near
    moves = []
    for h in range(2):
        moves += [
            (st_pj.at[h, pl.ds(0, near)], pj.at[h, z, pl.ds(0, near)], 0, h, low),
            (st_pj.at[h, pl.ds(0, near)], pj.at[h, z, pl.ds(near, near)], 1, h, high),
            (st_pj.at[h, near], pj.at[h, z, 2 * near], 2, h, low == low_has_far),
            (st_v.at[h], vv.at[h, z, pl.ds(0, 8)], 3, h, low),
            (st_v.at[h], vv.at[h, z, pl.ds(8, 8)], 4, h, high),
            (trans.at[pl.ds(h * HALF, HALF)], av.at[h, z], 5, h, high),
        ]

    def shift(source, target, k, h):
        return pltpu.make_async_remote_copy(
            src_ref=source, dst_ref=target, send_sem=shift_send.at[k, h], recv_sem=shift_recv.at[k],
            device_id=(target_base + h, z), device_id_type=MESH,
        )

    for source, target, k, h, active in moves:
        here = target_base + h == t

        @pl.when(jnp.logical_and(active, here))
        def _():
            pltpu.make_async_copy(source, target, shift_recv.at[k]).start()

        @pl.when(jnp.logical_and(active, jnp.logical_not(here)))
        def _():
            shift(source, target, k, h).start()

    await_bytes(pj.at[core, z, pl.ds(0, near)], shift_recv.at[0])
    await_bytes(pj.at[core, z, pl.ds(near, near)], shift_recv.at[1])
    await_bytes(pj.at[core, z, 2 * near], shift_recv.at[2])
    await_bytes(vv.at[core, z, pl.ds(0, 8)], shift_recv.at[3])
    await_bytes(vv.at[core, z, pl.ds(8, 8)], shift_recv.at[4])

    def part(kind, h, owner):
        if kind == 0:
            return pj.at[h, owner, pl.ds(0, near)]
        if kind == 1:
            return pj.at[h, owner, pl.ds(near, near + 1)]
        if kind == 2:
            return vv.at[h, owner]
        return av.at[h, owner, pl.ds((kind - 3) * (HALF // 2), HALF // 2)]

    def parts(kind, h, count):
        if kind == 0:
            return pj.at[h, pl.ds(0, count), pl.ds(0, near)]
        if kind == 1:
            return pj.at[h, pl.ds(0, count), pl.ds(near, near + 1)]
        if kind == 2:
            return vv.at[h, pl.ds(0, count)]
        return av.at[h, pl.ds(0, count), pl.ds((kind - 3) * (HALF // 2), HALF // 2)]

    def copy(kind, owner, way):
        device = ((t, up), (t, down), (partner, z))[way]
        ref = part(kind, core, owner)
        return pltpu.make_async_remote_copy(
            src_ref=ref, dst_ref=ref, send_sem=send.at[kind, way], recv_sem=recv.at[kind, core, owner],
            device_id=device, device_id_type=MESH,
        )

    def arrived(kind, h, owner):
        await_bytes(part(kind, h, owner), recv.at[kind, h, owner])

    def begin(kinds):
        for kind in kinds:
            for way in range(3):
                copy(kind, z, way).start()

    def hop(kinds, step):
        before, after = lax.rem(z - step + Z, Z), lax.rem(z + step, Z)
        for kind in kinds:
            arrived(kind, core, before)

            @pl.when(jnp.logical_or(step < H - 1, core == 0))
            def _():
                copy(kind, before, 0).start()

            copy(kind, before, 2).start()
            arrived(kind, core, after)

            @pl.when(jnp.logical_or(step < H - 1, core == 1))
            def _():
                copy(kind, after, 1).start()

            copy(kind, after, 2).start()

    def last_hop(kinds):
        far = lax.rem(z + H, Z)
        for kind in kinds:
            arrived(kind, core, far)
            copy(kind, far, 2).start()

    def completed(step):
        owner = jnp.where(lax.rem(step + z, 2) == 1, lax.rem(z + step, Z), lax.rem(z - step + Z, Z))
        return owner // 2

    def store(index, row, column, block):
        top, rest = split(block)
        where = (pl.ds(pl.multiple_of(row * LANES, LANES), LANES), pl.ds(pl.multiple_of(column * LANES, LANES), LANES))
        (p_high, j_high)[index][where] = top
        (p_low, j_low)[index][where] = rest

    def unpack(step):
        row = completed(step)
        for owner in (2 * row, 2 * row + 1):
            for kind in (0, 1, 2):
                arrived(kind, 1 - core, owner)

        def block(k):
            return jnp.concatenate(
                [pj[0, 2 * row, k], pj[1, 2 * row, k], pj[0, 2 * row + 1, k], pj[1, 2 * row + 1, k]], axis=0
            )

        for index in range(2):
            for k in range(near):
                column = lax.rem(row + k, supers)
                value = block(index * near + k)
                store(index, row, column, value)
                if k:
                    store(index, column, row, value.T)
        column = lax.rem(row + near, supers)
        value = block(2 * near)
        for index in range(2):
            @pl.when((row < near) == (index == 0))
            def _():
                store(index, row, column, value)
                store(index, column, row, value.T)

    matrices = (0, 1, 2)
    states = (3, 4)
    lag = min(LAG, H - 1)
    begin(matrices)

    def first_steps(step, _):
        hop(matrices, step)

        @pl.when(step > 1)
        def _():
            unpack(step - 1)

        return 0

    lax.fori_loop(1, lag + 1, first_steps, 0)
    await_bytes(av.at[core, z], shift_recv.at[5])
    begin(states)

    def later_steps(step, _):
        hop(matrices, step)
        hop(states, step - lag)
        unpack(step - 1)
        return 0

    lax.fori_loop(lag + 1, H, later_steps, 0)
    last_hop(matrices)
    pending = list(range(H - lag, H))

    def next_hop():
        if pending:
            hop(states, pending.pop(0))

    next_hop()
    unpack(H - 1)
    unpack(H)
    pj_save = pltpu.make_async_copy(pj, pj_out, out_sem.at[0])
    v_save = pltpu.make_async_copy(vv, v_out, out_sem.at[1])
    pj_save.start()
    v_save.start()

    width = min(256, size)
    unit = (
        lax.broadcasted_iota(jnp.int32, (width, width), 0) == lax.broadcasted_iota(jnp.int32, (width, width), 1)
    ).astype(F32)
    for q in range(size // width):
        columns = slice(q * width, (q + 1) * width)
        product = dot(p_high[...], j_high[:, columns])
        corner = product[columns]
        inverse = 1.0 / (1.0 + jnp.sum(corner * unit, axis=0, keepdims=True))
        scale[:, columns] = jnp.broadcast_to(inverse, (8, width))
        series[:, columns] = (-product * inverse).astype(BF16)
        series[columns, columns] = (unit - (unit + corner) * inverse).astype(BF16)
    next_hop()

    inverse = scale[0:1]

    def approximate(value):
        first = value * inverse
        result = first
        for _ in range(3):
            result = first + dot(result.astype(BF16), series[...])
        return result

    def exact(value, top, rest):
        count = value.shape[0]
        big, small = split(value)
        both = dot(jnp.concatenate([big, small], axis=0), top[...])
        return both[:count] + both[count:] + dot(big, rest[...])

    def vector_row(k):
        tiles = []
        for s in range(supers):
            tiles.append(
                (vv[0, 2 * s, pl.ds(8 * k, 8)] + vv[1, 2 * s, pl.ds(8 * k, 8)])
                + (vv[0, 2 * s + 1, pl.ds(8 * k, 8)] + vv[1, 2 * s + 1, pl.ds(8 * k, 8)])
            )
        return jnp.concatenate(tiles, axis=1)

    target = av[core, z]
    x = approximate(target)
    stacked = exact(jnp.concatenate([x, vector_row(1)], axis=0), p_high, p_low)
    y = stacked[:HALF]
    combined = vector_row(0) + stacked[HALF:]
    next_hop()
    residual = target - x - exact(y, j_high, j_low)
    change = approximate(residual)
    x = x + change
    moved = exact(change, p_high, p_low)
    y = y + moved
    residual = residual - change - exact(moved, j_high, j_low)
    while pending:
        next_hop()
    last_hop(states)
    change = approximate(residual)
    x = x + change
    moved = dot(change.astype(BF16), p_high[...])
    y = y + moved
    residual = residual - change - dot(moved.astype(BF16), j_high[...])
    error = jnp.sum(residual * residual)
    norm = jnp.sum(target * target)
    good = jnp.where(error <= (TOLERANCE * TOLERANCE) * norm, 1.0, 0.0).astype(F32)
    small_out[0:8] = jnp.zeros((8, LANES), F32)
    small_out[0:8, 0:HALF] = lax.dot_general(
        combined, x, (((1,), (1,)), ((), ())), precision=HIGHEST, preferred_element_type=F32
    )
    small_out[8:16] = jnp.broadcast_to(good, (8, LANES))

    y_high, y_low = split(y)
    y_both = jnp.concatenate([y_high, y_low], axis=0)

    def product_steps(step, _):
        row = completed(step)
        for owner in (2 * row, 2 * row + 1):
            for kind in states:
                arrived(kind, 1 - core, owner)
        block = jnp.concatenate(
            [av[0, 2 * row], av[1, 2 * row], av[0, 2 * row + 1], av[1, 2 * row + 1]], axis=0
        )
        top, rest = split(block)
        both = dot_nt(y_both, top)
        rows_out[:, pl.ds(pl.multiple_of(row * LANES, LANES), LANES)] = (
            both[:HALF] + both[HALF:] + dot_nt(y_high, rest)
        )
        return 0

    lax.fori_loop(1, H + 1, product_steps, 0)
    a_save = pltpu.make_async_copy(av, a_out, out_sem.at[2])
    a_save.start()

    for kind in matrices + states:
        await_bytes(parts(kind, core, Z), send.at[kind, 2])
        for way in range(2):
            @pl.when(core == way)
            def _():
                await_bytes(parts(kind, core, H), send.at[kind, way])

            @pl.when(core != way)
            def _():
                await_bytes(parts(kind, core, H - 1), send.at[kind, way])
    for source, target, k, h, active in moves:
        @pl.when(jnp.logical_and(active, target_base + h != t))
        def _():
            shift(source, target, k, h).wait_send()
    pj_save.wait()
    v_save.wait()
    a_save.wait()


def return_kernel(T, rows, small, cov, mean, cov_out, mean_out, rows_in, small_in, recv, send):
    t, z, core, low, base_low, base_high = place(T)
    high = jnp.logical_not(low)
    owner = jnp.where(low, base_high, base_high + 1)
    partner = t + 1 - 2 * core
    opposite = jnp.where(low, base_high, base_low)
    barrier = pltpu.get_barrier_semaphore()
    for device in ((partner, z), (opposite, z), (opposite + 1, z)):
        pl.semaphore_signal(barrier, inc=1, device_id=device, device_id_type=MESH)
    pl.semaphore_wait(barrier, 3)
    moves = ((rows, rows_in.at[core], 0), (small.at[pl.ds(0, 8)], small_in.at[core], 1))
    here = owner == t

    def back(source, target, k):
        return pltpu.make_async_remote_copy(
            src_ref=source, dst_ref=target, send_sem=send.at[k], recv_sem=recv.at[k, core],
            device_id=(owner, z), device_id_type=MESH,
        )

    for source, target, k in moves:
        @pl.when(here)
        def _():
            pltpu.make_async_copy(source, target, recv.at[k, core]).start()

        @pl.when(jnp.logical_not(here))
        def _():
            back(source, target, k).start()

    @pl.when(low)
    def _():
        cov_out[...] = cov[...]
        mean_out[...] = mean[...]

    @pl.when(high)
    def _():
        for h in range(2):
            await_bytes(rows_in.at[h], recv.at[0, h])
            cov_out[h * HALF : (h + 1) * HALF] = rows_in[h] + cov[h * HALF : (h + 1) * HALF]
            await_bytes(small_in.at[h], recv.at[1, h])
        mean_out[...] = mean[...] + jnp.concatenate([small_in[0, 0:1, 0:HALF], small_in[1, 0:1, 0:HALF]], axis=1)

    for source, target, k in moves:
        @pl.when(jnp.logical_not(here))
        def _():
            back(source, target, k).wait_send()


def by_factors(operands):
    pj, av, vv = operands
    Z = av.shape[1]
    supers = Z // 2
    near = supers // 2
    size = Z * ROWS
    core = lax.rem(lax.axis_index("tm"), 2)
    z = lax.axis_index("panel")
    packed = pj.transpose(1, 0, 3, 2, 4).reshape(supers, LANES, 2 * near + 1, LANES).transpose(0, 2, 1, 3)

    def whole(index):
        grid = [[None] * supers for _ in range(supers)]
        for row in range(supers):
            for k in range(near + 1):
                if k == near and (row < near) != (index == 0):
                    continue
                block = packed[row, 2 * near if k == near else index * near + k]
                column = (row + k) % supers
                grid[row][column] = block
                if k:
                    grid[column][row] = block.T
        return jnp.concatenate([jnp.concatenate(row, axis=1) for row in grid], axis=0)

    cov, info = whole(0), whole(1)
    rows = av.transpose(1, 0, 2, 3).reshape(size, size)
    tiles = vv[:, :, ::8].sum(axis=0).reshape(supers, 2, 2, LANES).sum(axis=1)
    mean, infovec = tiles[:, 0].reshape(size), tiles[:, 1].reshape(size)
    mm = functools.partial(jnp.dot, precision=HIGHEST)
    lower_factor = jnp.linalg.cholesky(cov)
    inner = jnp.eye(size, dtype=F32) + mm(lower_factor.T, mm(info, lower_factor))
    inner_factor = jnp.linalg.cholesky(inner)
    mixed = mm(rows, lower_factor)
    factor = jax.scipy.linalg.solve_triangular(inner_factor, mixed.T, lower=True).T
    mine = lax.dynamic_slice_in_dim(factor, z * ROWS + core * HALF, HALF, 0)
    mixed_mine = lax.dynamic_slice_in_dim(mixed, z * ROWS + core * HALF, HALF, 0)
    right = jax.scipy.linalg.solve_triangular(lower_factor, mean, lower=True) + mm(infovec, lower_factor)
    weight = jax.scipy.linalg.cho_solve((inner_factor, True), right)
    small = jnp.zeros((16, LANES), F32).at[0:8, 0:HALF].set(mm(mixed_mine, weight)[None])
    return mm(mine, factor.T), small


def solution(mesh):
    T, Z = mesh.shape["tm"], mesh.shape["panel"]
    near = Z // 4
    size = Z * ROWS
    vmem = pl.BlockSpec(memory_space=pltpu.VMEM)
    hbm = pl.BlockSpec(memory_space=pl.ANY)
    dma = pltpu.SemaphoreType.DMA
    pj_shape = (2, Z, 2 * near + 1, HALF, LANES)
    a_shape = (2, Z, HALF, size)
    v_shape = (2, Z, 16, LANES)
    struct = lambda *shape: jax.ShapeDtypeStruct(shape, F32)

    def body(elem_trans, elem_cov, elem_info, elem_mean, elem_infovec):
        rows, small, pj, av, vv = pl.pallas_call(
            functools.partial(solve_kernel, T, Z),
            name="gather_and_solve",
            out_shape=(struct(HALF, size), struct(16, LANES), struct(*pj_shape), struct(*a_shape), struct(*v_shape)),
            in_specs=[vmem] * 5,
            out_specs=(vmem, vmem, hbm, hbm, hbm),
            scratch_shapes=[
                pltpu.VMEM(pj_shape, F32),
                pltpu.VMEM(a_shape, F32),
                pltpu.VMEM(v_shape, F32),
                pltpu.VMEM((2, near + 1, HALF, LANES), F32),
                pltpu.VMEM((2, 8, LANES), F32),
            ]
            + [pltpu.VMEM((size, size), BF16)] * 5
            + [
                pltpu.VMEM((8, size), F32),
                dma((5, 2, Z)),
                dma((5, 3)),
                dma((6,)),
                dma((6, 2)),
                dma((3,)),
            ],
            compiler_params=pltpu.CompilerParams(
                collective_id=0, has_side_effects=True, vmem_limit_bytes=48 * 2**20
            ),
        )(elem_trans[0], elem_cov[0], elem_info[0], elem_mean, elem_infovec)
        rows, small = lax.cond(
            small[8, 0] > 0.5, lambda operands: (rows, small), by_factors, (pj, av, vv)
        )
        new_cov, new_mean = pl.pallas_call(
            functools.partial(return_kernel, T),
            name="rows_to_owner",
            out_shape=(struct(ROWS, size), struct(1, ROWS)),
            in_specs=[vmem] * 4,
            out_specs=(vmem, vmem),
            scratch_shapes=[
                pltpu.VMEM((2, HALF, size), F32),
                pltpu.VMEM((2, 8, LANES), F32),
                dma((2, 2)),
                dma((2,)),
            ],
            compiler_params=pltpu.CompilerParams(collective_id=1, has_side_effects=True),
        )(rows, small, elem_cov[0], elem_mean)
        return new_cov[None], new_mean

    matrix, line = P("tm", "panel", None), P("tm", "panel")
    return jax.shard_map(
        body,
        mesh=mesh,
        in_specs=(matrix, matrix, matrix, line, line),
        out_specs=(matrix, line),
        check_vma=False,
    )
```

```python
import functools

import jax
import jax.numpy as jnp
from jax import lax
from jax.experimental import pallas as pl
from jax.experimental.pallas import tpu as pltpu
from jax.sharding import PartitionSpec as P

MESH = pl.DeviceIdType.MESH
HIGHEST = lax.Precision.HIGHEST
F32 = jnp.float32
BF16 = jnp.bfloat16
ROWS = 64
HALF = 32
LANES = 128
LAG = 2
CHUNKS = 2
LIMIT = 0.16


def split(value):
    high = value.astype(BF16)
    return high, (value - high.astype(F32)).astype(BF16)


def dot(left, right):
    return jnp.dot(left, right, preferred_element_type=F32)


def dot_nt(left, right):
    return lax.dot_general(left, right, (((1,), (1,)), ((), ())), preferred_element_type=F32)


def place(T):
    t = lax.axis_index("tm")
    z = lax.axis_index("panel")
    distance = T // 2
    core = lax.rem(t, 2)
    low = t < distance
    base_low = lax.rem(t, distance) - core
    base_high = base_low + distance
    return t, z, core, low, base_low, base_high


def await_bytes(ref, sem):
    pltpu.make_async_copy(ref, ref, sem).wait()


def solve_kernel(
    T, Z,
    trans, cov, info, mean, infovec,
    cov_out, mean_out, good_out,
    pj, av, vec, st_v, state_cov, rows_in, small_in, rows, small, good,
    p_high, p_low, j_high, j_low, series, square, fourth, scale,
    recv, send, shift_recv, shift_send, local, back_recv, back_send, good_recv, good_send,
):
    t, z, core, low, base_low, base_high = place(T)
    supers = Z // 2
    near = supers // 2
    H = Z // 2
    size = Z * ROWS
    partner = t + 1 - 2 * core
    opposite = jnp.where(low, base_high, base_low)
    up, down = lax.rem(z + 1, Z), lax.rem(z + Z - 1, Z)

    fast = min(4, T // 2)
    slow = T // 2 // fast
    chip = t // 2
    chip_slow, chip_fast = chip // fast, lax.rem(chip, fast)
    fast_peers = [(chip_slow * fast + lax.rem(chip_fast + k, fast)) * 2 + core for k in range(1, fast)]
    slow_peers = [(lax.rem(chip_slow + k, slow) * fast + chip_fast) * 2 + core for k in range(1, slow)]
    devices = [(t, up), (t, down), (partner, z), (opposite, z), (opposite + 1, z)]
    devices += [(peer, z) for peer in fast_peers + slow_peers]
    barrier = pltpu.get_barrier_semaphore()
    for device in devices:
        pl.semaphore_signal(barrier, inc=1, device_id=device, device_id_type=MESH)

    fetches = [
        pltpu.make_async_copy(source, target, local.at[k])
        for k, (source, target) in enumerate(((mean, vec.at[0]), (infovec, vec.at[1]), (cov, state_cov)))
    ]
    for fetch in fetches:
        fetch.start()
    fetches[0].wait()
    fetches[1].wait()
    vector = jnp.where(low, vec[0], vec[1])
    nothing = jnp.zeros_like(vector)
    vector = jnp.where(
        lax.rem(z, 2) == 0,
        jnp.concatenate([vector, nothing], axis=1),
        jnp.concatenate([nothing, vector], axis=1),
    )
    lane = lax.broadcasted_iota(jnp.int32, (8, LANES), 1)
    for h in range(2):
        start = lax.rem(z, 2) * ROWS + h * HALF
        mine = jnp.logical_and(lane >= start, lane < start + HALF)
        st_v[h] = jnp.where(mine, jnp.broadcast_to(vector, (8, LANES)), 0.0)
    own_super = z // 2
    pl.semaphore_wait(barrier, len(devices))

    target_base = jnp.where(core == 0, base_low, base_high)
    high = jnp.logical_not(low)
    low_has_far = own_super < near
    far = 2 * near * HALF
    tail = far + HALF
    moves = []
    for h in range(2):
        here_rows = pl.ds(h * HALF, HALF)
        for k in range(near + 1):
            column = pl.ds(pl.multiple_of(lax.rem(own_super + k, supers) * LANES, LANES), LANES)
            if k < near:
                moves.append((cov.at[here_rows, column], pj.at[h, z, pl.ds(k * HALF, HALF)], 0, h, low))
                moves.append((info.at[here_rows, column], pj.at[h, z, pl.ds((near + k) * HALF, HALF)], 1, h, high))
            else:
                block = pj.at[h, z, pl.ds(far, HALF)]
                moves.append((cov.at[here_rows, column], block, 2, h, jnp.logical_and(low, low_has_far)))
                moves.append(
                    (info.at[here_rows, column], block, 2, h, jnp.logical_and(high, jnp.logical_not(low_has_far)))
                )
        moves.append((st_v.at[h], pj.at[h, z, pl.ds(tail, 8)], 3, h, low))
        moves.append((st_v.at[h], pj.at[h, z, pl.ds(tail + 8, 8)], 4, h, high))
    state_moves = [(trans.at[pl.ds(h * HALF, HALF)], av.at[h, z], 5, h, high) for h in range(2)]

    def shift(source, target, k, h):
        return pltpu.make_async_remote_copy(
            src_ref=source, dst_ref=target, send_sem=shift_send.at[k, h], recv_sem=shift_recv.at[k],
            device_id=(target_base + h, z), device_id_type=MESH,
        )

    def start_moves(chosen):
        for source, target, k, h, active in chosen:
            here = target_base + h == t

            @pl.when(jnp.logical_and(active, here))
            def _():
                pltpu.make_async_copy(source, target, shift_recv.at[k]).start()

            @pl.when(jnp.logical_and(active, jnp.logical_not(here)))
            def _():
                shift(source, target, k, h).start()

    start_moves(moves)
    await_bytes(pj.at[core, z, pl.ds(0, near * HALF)], shift_recv.at[0])
    await_bytes(pj.at[core, z, pl.ds(near * HALF, near * HALF)], shift_recv.at[1])
    await_bytes(pj.at[core, z, pl.ds(far, HALF)], shift_recv.at[2])
    await_bytes(pj.at[core, z, pl.ds(tail, 8)], shift_recv.at[3])
    await_bytes(pj.at[core, z, pl.ds(tail + 8, 8)], shift_recv.at[4])

    def part(kind, h, owner):
        buffer, rows_each = ((pj, (tail + 16) // CHUNKS), (av, HALF // CHUNKS))[kind // CHUNKS]
        return buffer.at[h, owner, pl.ds(kind % CHUNKS * rows_each, rows_each)]

    def parts(kind, h, count):
        buffer, rows_each = ((pj, (tail + 16) // CHUNKS), (av, HALF // CHUNKS))[kind // CHUNKS]
        return buffer.at[h, pl.ds(0, count), pl.ds(kind % CHUNKS * rows_each, rows_each)]

    def copy(kind, owner, way):
        device = ((t, up), (t, down), (partner, z))[way]
        ref = part(kind, core, owner)
        return pltpu.make_async_remote_copy(
            src_ref=ref, dst_ref=ref, send_sem=send.at[kind, way], recv_sem=recv.at[kind, core, owner],
            device_id=device, device_id_type=MESH,
        )

    def arrived(kind, h, owner):
        await_bytes(part(kind, h, owner), recv.at[kind, h, owner])

    def begin(kinds):
        for kind in kinds:
            for way in range(3):
                copy(kind, z, way).start()

    def hop(kinds, step):
        before, after = lax.rem(z - step + Z, Z), lax.rem(z + step, Z)
        for kind in kinds:
            arrived(kind, core, before)

            @pl.when(jnp.logical_or(step < H - 1, core == 0))
            def _():
                copy(kind, before, 0).start()

            arrived(kind, core, after)

            @pl.when(jnp.logical_or(step < H - 1, core == 1))
            def _():
                copy(kind, after, 1).start()

            copy(kind, before, 2).start()
            copy(kind, after, 2).start()

    def last_hop(kinds):
        far = lax.rem(z + H, Z)
        for kind in kinds:
            arrived(kind, core, far)
            copy(kind, far, 2).start()

    def completed(step):
        owner = jnp.where(lax.rem(step + z, 2) == 1, lax.rem(z + step, Z), lax.rem(z - step + Z, Z))
        return owner // 2

    def store(index, row, column, block):
        top, rest = split(block)
        where = (pl.ds(pl.multiple_of(row * LANES, LANES), LANES), pl.ds(pl.multiple_of(column * LANES, LANES), LANES))
        (p_high, j_high)[index][where] = top
        (p_low, j_low)[index][where] = rest

    def unpack(step):
        row = completed(step)
        for owner in (2 * row, 2 * row + 1):
            for kind in matrices:
                arrived(kind, 1 - core, owner)

        def block(k):
            return jnp.concatenate(
                [pj[h, 2 * row + i, k * HALF : (k + 1) * HALF] for i in range(2) for h in range(2)], axis=0
            )

        for index in range(2):
            for k in range(near):
                column = lax.rem(row + k, supers)
                value = block(index * near + k)
                store(index, row, column, value)
                if k:
                    store(index, column, row, value.T)
        column = lax.rem(row + near, supers)
        value = block(2 * near)
        for index in range(2):
            @pl.when((row < near) == (index == 0))
            def _():
                store(index, row, column, value)
                store(index, column, row, value.T)

    matrices, states = tuple(range(CHUNKS)), tuple(range(CHUNKS, 2 * CHUNKS))
    lag = min(LAG, H - 1)
    begin(matrices)
    start_moves(state_moves)

    def first_steps(step, _):
        hop(matrices, step)

        @pl.when(step > 1)
        def _():
            unpack(step - 1)

        return 0

    lax.fori_loop(1, lag + 1, first_steps, 0)
    await_bytes(av.at[core, z], shift_recv.at[5])
    begin(states)

    def later_steps(step, _):
        hop(matrices, step)
        hop(states, step - lag)
        unpack(step - 1)
        return 0

    lax.fori_loop(lag + 1, H, later_steps, 0)
    last_hop(matrices)
    pending = list(range(H - lag, H))

    def next_hop():
        if pending:
            hop(states, pending.pop(0))

    next_hop()
    unpack(H - 1)
    unpack(H)
    width = min(256, size)
    unit = (
        lax.broadcasted_iota(jnp.int32, (width, width), 0) == lax.broadcasted_iota(jnp.int32, (width, width), 1)
    ).astype(F32)
    for q in range(size // width):
        columns = slice(q * width, (q + 1) * width)
        product = dot(p_high[...], j_high[:, columns])
        corner = product[columns]
        inverse = 1.0 / (1.0 + jnp.sum(corner * unit, axis=0, keepdims=True))
        scale[:, columns] = jnp.broadcast_to(inverse, (8, width))
        series[:, columns] = (-product * inverse).astype(BF16)
        series[columns, columns] = (unit - (unit + corner) * inverse).astype(BF16)
    next_hop()
    total = 0.0
    for source, target in ((series, square), (square, fourth)):
        for q in range(size // width):
            columns = slice(q * width, (q + 1) * width)
            product = dot(source[...], source[:, columns])
            target[:, columns] = product.astype(BF16)
            if target is fourth:
                total = total + jnp.sum(product * product)
        next_hop()

    def agree(value, axis, index, peers):
        good[axis, index] = value
        copies = [
            pltpu.make_async_remote_copy(
                src_ref=good.at[axis, index], dst_ref=good.at[axis, index], send_sem=good_send.at[axis, k],
                recv_sem=good_recv.at[axis, index], device_id=(peer, z), device_id_type=MESH,
            )
            for k, peer in enumerate(peers)
        ]
        for one in copies:
            one.start()

        def result():
            count = len(peers) + 1
            for k in range(1, count):
                other = lax.rem(index + k, count)
                await_bytes(good.at[axis, other], good_recv.at[axis, other])
            value = good[axis, 0]
            for k in range(1, count):
                value = jnp.minimum(value, good[axis, k])
            for one in copies:
                one.wait_send()
            return value

        return result

    bounded = jnp.where(total <= LIMIT * LIMIT, 1.0, 0.0).astype(F32)
    fast_result = agree(jnp.broadcast_to(bounded, (8, LANES)), 0, chip_fast, fast_peers)

    inverse = scale[0:1]

    def approximate(value):
        result = value * inverse
        for factor in (series, square, fourth):
            result = result + dot(result.astype(BF16), factor[...])
        return result

    def exact(value, top, rest):
        count = value.shape[0]
        big, small = split(value)
        both = dot(jnp.concatenate([big, small], axis=0), top[...])
        return both[:count] + both[count:] + dot(big, rest[...])

    def vector_row(k):
        at = slice(tail + 8 * k, tail + 8 * k + 8)
        tiles = [
            (pj[0, 2 * s, at] + pj[1, 2 * s, at]) + (pj[0, 2 * s + 1, at] + pj[1, 2 * s + 1, at])
            for s in range(supers)
        ]
        return jnp.concatenate(tiles, axis=1)

    target = av[core, z]
    x = approximate(target)
    stacked = exact(jnp.concatenate([x, vector_row(1)], axis=0), p_high, p_low)
    y = stacked[:HALF]
    combined = vector_row(0) + stacked[HALF:]
    next_hop()
    residual = target - x - exact(y, j_high, j_low)
    change = approximate(residual)
    x = x + change
    moved = exact(change, p_high, p_low)
    y = y + moved
    residual = residual - change - exact(moved, j_high, j_low)
    slow_result = agree(fast_result(), 1, chip_slow, slow_peers)
    while pending:
        next_hop()
    last_hop(states)
    change = approximate(residual)
    x = x + change
    moved = dot(change.astype(BF16), p_high[...])
    y = y + moved
    small[...] = jnp.zeros((8, LANES), F32)
    small[:, 0:HALF] = lax.dot_general(
        combined, x, (((1,), (1,)), ((), ())), precision=HIGHEST, preferred_element_type=F32
    )
    owner_device = jnp.where(low, base_high, base_high + 1)
    mine = owner_device == t

    def give(source, target, arrival, departure):
        @pl.when(mine)
        def _():
            pltpu.make_async_copy(source, target, arrival).start()

        @pl.when(jnp.logical_not(mine))
        def _():
            pltpu.make_async_remote_copy(
                src_ref=source, dst_ref=target, send_sem=departure, recv_sem=arrival,
                device_id=(owner_device, z), device_id_type=MESH,
            ).start()

    give(small, small_in.at[core], back_recv.at[supers, core], back_send.at[1])

    y_high, y_low = split(y)
    y_both = jnp.concatenate([y_high, y_low], axis=0)

    def product_steps(step, _):
        row = completed(step)
        for owner in (2 * row, 2 * row + 1):
            for kind in states:
                arrived(kind, 1 - core, owner)
        block = jnp.concatenate(
            [av[0, 2 * row], av[1, 2 * row], av[0, 2 * row + 1], av[1, 2 * row + 1]], axis=0
        )
        top, rest = split(block)
        both = dot_nt(y_both, top)
        rows[row] = both[:HALF] + both[HALF:] + dot_nt(y_high, rest)
        give(rows.at[row], rows_in.at[core, row], back_recv.at[row, core], back_send.at[0])
        return 0

    lax.fori_loop(1, H + 1, product_steps, 0)
    good_out[...] = slow_result()
    fetches[2].wait()

    @pl.when(low)
    def _():
        cov_out[...] = state_cov[...]
        mean_out[...] = vec[0]

    @pl.when(high)
    def _():
        for step in range(1, H + 1):
            row = completed(step)
            column = pl.ds(pl.multiple_of(row * LANES, LANES), LANES)
            for h in range(2):
                await_bytes(rows_in.at[h, row], back_recv.at[row, h])
                cov_out[h * HALF : (h + 1) * HALF, column] = (
                    rows_in[h, row] + state_cov[h * HALF : (h + 1) * HALF, column]
                )
        for h in range(2):
            await_bytes(small_in.at[h], back_recv.at[supers, h])
        mean_out[...] = vec[0] + jnp.concatenate([small_in[0, 0:1, 0:HALF], small_in[1, 0:1, 0:HALF]], axis=1)

    for kind in matrices + states:
        await_bytes(parts(kind, core, Z), send.at[kind, 2])
        for way in range(2):
            @pl.when(core == way)
            def _():
                await_bytes(parts(kind, core, H), send.at[kind, way])

            @pl.when(core != way)
            def _():
                await_bytes(parts(kind, core, H - 1), send.at[kind, way])
    for h in range(2):
        away = target_base + h != t
        for k, count in ((0, near), (1, near), (2, 1)):
            side = (low, high, low == low_has_far)[k]

            @pl.when(jnp.logical_and(side, away))
            def _():
                await_bytes(pj.at[h, 0, pl.ds(0, count * HALF)], shift_send.at[k, h])

        for k, side in ((3, low), (4, high)):
            @pl.when(jnp.logical_and(side, away))
            def _():
                await_bytes(st_v.at[h], shift_send.at[k, h])

        @pl.when(jnp.logical_and(high, away))
        def _():
            await_bytes(av.at[h, 0], shift_send.at[5, h])

    @pl.when(jnp.logical_not(mine))
    def _():
        await_bytes(rows, back_send.at[0])
        await_bytes(small, back_send.at[1])


def from_behind(array, axis, by):
    devices = lax.axis_size(axis)
    pairs = [(i, i + by) for i in range(devices) if 0 <= i + by < devices]
    return lax.ppermute(array, axis, pairs)


def block_cholesky(matrix):
    state_count = matrix.shape[0]
    split = state_count // 2
    top_left = matrix[:split, :split]
    bottom_left = matrix[split:, :split]
    bottom_right = matrix[split:, split:]
    first_factor = jnp.linalg.cholesky(top_left)
    side_block = jax.scipy.linalg.solve_triangular(first_factor, bottom_left.T, lower=True).T
    schur_block = bottom_right - jnp.dot(side_block, side_block.T, precision=HIGHEST)
    second_factor = jnp.linalg.cholesky(schur_block)
    upper_rows = jnp.concatenate(
        [first_factor, jnp.zeros((split, state_count - split), jnp.float32)], axis=1
    )
    lower_rows = jnp.concatenate([side_block, second_factor], axis=1)
    return jnp.concatenate([upper_rows, lower_rows], axis=0)


def by_factors(elem_trans, elem_cov, elem_info, elem_mean, elem_infovec):
    distance = lax.axis_size("tm") // 2
    transition = elem_trans[0]
    covariance = elem_cov[0]
    information = elem_info[0]
    state_mean = elem_mean[0]
    info_vector = elem_infovec[0]
    state_count = covariance.shape[1]
    upper = lax.axis_index("tm") >= distance
    identity_matrix = jnp.eye(state_count, dtype=jnp.float32)
    prev_cov, prev_mean = from_behind((covariance, state_mean), "tm", distance)
    whole_cov, whole_mean = (
        lax.all_gather(prev_cov, "panel", axis=0, tiled=True),
        lax.all_gather(prev_mean, "panel", axis=0, tiled=True),
    )
    whole_cov = jnp.where(upper, whole_cov, identity_matrix)
    lower_factor = block_cholesky(whole_cov)
    coupling_rows = jnp.dot(information, lower_factor, precision=HIGHEST)
    coupling, whole_vector = (
        lax.all_gather(coupling_rows, "panel", axis=0, tiled=True),
        lax.all_gather(info_vector, "panel", axis=0, tiled=True),
    )
    inner = identity_matrix + jnp.dot(lower_factor.T, coupling, precision=HIGHEST)
    inner_factor = block_cholesky(inner)
    mixed_rows = jnp.dot(transition, lower_factor, precision=HIGHEST)
    factor_part = jax.scipy.linalg.solve_triangular(inner_factor, mixed_rows.T, lower=True).T
    combined_rows = (
        jnp.dot(
            factor_part,
            lax.all_gather(factor_part, "panel", axis=0, tiled=True).T,
            precision=HIGHEST,
        )
        + covariance
    )
    right_side = jax.scipy.linalg.solve_triangular(lower_factor, whole_mean, lower=True)
    right_side = right_side + jnp.dot(whole_vector, lower_factor, precision=HIGHEST)
    weight = jax.scipy.linalg.cho_solve((inner_factor, True), right_side)
    combined_mean = jnp.dot(mixed_rows, weight, precision=HIGHEST) + state_mean
    result_cov = jnp.where(upper, combined_rows, covariance)
    result_mean = jnp.where(upper, combined_mean, state_mean)
    return (result_cov[None], result_mean[None])


def solution(mesh):
    T, Z = mesh.shape["tm"], mesh.shape["panel"]
    near = Z // 4
    size = Z * ROWS
    vmem = pl.BlockSpec(memory_space=pltpu.VMEM)
    hbm = pl.BlockSpec(memory_space=pltpu.HBM)
    dma = pltpu.SemaphoreType.DMA
    supers = Z // 2
    struct = lambda *shape: jax.ShapeDtypeStruct(shape, F32)
    scratch = lambda *shape: pltpu.VMEM(shape, F32)

    def body(*arrays):
        elem_trans, elem_cov, elem_info, elem_mean, elem_infovec = arrays
        new_cov, new_mean, good = pl.pallas_call(
            functools.partial(solve_kernel, T, Z),
            name="gather_and_solve",
            out_shape=(struct(ROWS, size), struct(1, ROWS), struct(8, LANES)),
            in_specs=[hbm] * 5,
            out_specs=(vmem, vmem, vmem),
            scratch_shapes=[
                scratch(2, Z, (2 * near + 1) * HALF + 16, LANES),
                scratch(2, Z, HALF, size),
                scratch(2, 1, ROWS),
                scratch(2, 8, LANES),
                scratch(ROWS, size),
                scratch(2, supers, HALF, LANES),
                scratch(2, 8, LANES),
                scratch(supers, HALF, LANES),
                scratch(8, LANES),
                scratch(2, 4, 8, LANES),
            ]
            + [pltpu.VMEM((size, size), BF16)] * 7
            + [
                scratch(8, size),
                dma((2 * CHUNKS, 2, Z)),
                dma((2 * CHUNKS, 3)),
                dma((6,)),
                dma((6, 2)),
                dma((3,)),
                dma((supers + 1, 2)),
                dma((2,)),
                dma((2, 4)),
                dma((2, 4)),
            ],
            compiler_params=pltpu.CompilerParams(
                collective_id=0, has_side_effects=True, vmem_limit_bytes=48 * 2**20
            ),
        )(elem_trans[0], elem_cov[0], elem_info[0], elem_mean, elem_infovec)
        return lax.cond(
            good[0, 0] > 0.5, lambda *_: (new_cov[None], new_mean), by_factors, *arrays
        )

    matrix, line = P("tm", "panel", None), P("tm", "panel")
    return jax.shard_map(
        body,
        mesh=mesh,
        in_specs=(matrix, matrix, matrix, line, line),
        out_specs=(matrix, line),
        check_vma=False,
    )
```

```python
import functools

import jax
import jax.numpy as jnp
from jax import lax
from jax.experimental import pallas as pl
from jax.experimental.pallas import tpu as pltpu
from jax.sharding import PartitionSpec as P

MESH = pl.DeviceIdType.MESH
HIGHEST = lax.Precision.HIGHEST
F32 = jnp.float32
BF16 = jnp.bfloat16
ROWS = 64
HALF = 32
LANES = 128
LAG = 2
CHUNKS = 2
LIMIT = 0.16


def split(value):
    high = value.astype(BF16)
    return high, (value - high.astype(F32)).astype(BF16)


def dot(left, right):
    return jnp.dot(left, right, preferred_element_type=F32)


def dot_nt(left, right):
    return lax.dot_general(left, right, (((1,), (1,)), ((), ())), preferred_element_type=F32)


def place(T):
    t = lax.axis_index("tm")
    z = lax.axis_index("panel")
    distance = T // 2
    core = lax.rem(t, 2)
    low = t < distance
    base_low = lax.rem(t, distance) - core
    base_high = base_low + distance
    return t, z, core, low, base_low, base_high


def await_bytes(ref, sem):
    pltpu.make_async_copy(ref, ref, sem).wait()


def solve_kernel(
    T, Z,
    trans, cov, info, mean, infovec,
    cov_out, mean_out, good_out, pj_out, a_out,
    pj, av, vec, st_v, state_cov, rows_in, small_in, rows, small, good,
    p_high, p_low, j_high, j_low, series, square, fourth, scale,
    recv, send, shift_recv, shift_send, local, back_recv, back_send, good_recv, good_send, save,
):
    t, z, core, low, base_low, base_high = place(T)
    supers = Z // 2
    near = supers // 2
    H = Z // 2
    size = Z * ROWS
    partner = t + 1 - 2 * core
    opposite = jnp.where(low, base_high, base_low)
    up, down = lax.rem(z + 1, Z), lax.rem(z + Z - 1, Z)

    fast = min(4, T // 2)
    slow = T // 2 // fast
    chip = t // 2
    chip_slow, chip_fast = chip // fast, lax.rem(chip, fast)
    fast_peers = [(chip_slow * fast + lax.rem(chip_fast + k, fast)) * 2 + core for k in range(1, fast)]
    slow_peers = [(lax.rem(chip_slow + k, slow) * fast + chip_fast) * 2 + core for k in range(1, slow)]
    devices = [(t, up), (t, down), (partner, z), (opposite, z), (opposite + 1, z)]
    devices += [(peer, z) for peer in fast_peers + slow_peers]
    barrier = pltpu.get_barrier_semaphore()
    for device in devices:
        pl.semaphore_signal(barrier, inc=1, device_id=device, device_id_type=MESH)

    fetches = [
        pltpu.make_async_copy(source, target, local.at[k])
        for k, (source, target) in enumerate(((mean, vec.at[0]), (infovec, vec.at[1]), (cov, state_cov)))
    ]
    for fetch in fetches:
        fetch.start()
    fetches[0].wait()
    fetches[1].wait()
    vector = jnp.where(low, vec[0], vec[1])
    nothing = jnp.zeros_like(vector)
    vector = jnp.where(
        lax.rem(z, 2) == 0,
        jnp.concatenate([vector, nothing], axis=1),
        jnp.concatenate([nothing, vector], axis=1),
    )
    lane = lax.broadcasted_iota(jnp.int32, (8, LANES), 1)
    for h in range(2):
        start = lax.rem(z, 2) * ROWS + h * HALF
        mine = jnp.logical_and(lane >= start, lane < start + HALF)
        st_v[h] = jnp.where(mine, jnp.broadcast_to(vector, (8, LANES)), 0.0)
    own_super = z // 2
    pl.semaphore_wait(barrier, len(devices))

    target_base = jnp.where(core == 0, base_low, base_high)
    high = jnp.logical_not(low)
    low_has_far = own_super < near
    far = 2 * near * HALF
    tail = far + HALF
    moves = []
    for h in range(2):
        here_rows = pl.ds(h * HALF, HALF)
        for k in range(near + 1):
            column = pl.ds(pl.multiple_of(lax.rem(own_super + k, supers) * LANES, LANES), LANES)
            if k < near:
                moves.append((cov.at[here_rows, column], pj.at[h, z, pl.ds(k * HALF, HALF)], 0, h, low))
                moves.append((info.at[here_rows, column], pj.at[h, z, pl.ds((near + k) * HALF, HALF)], 1, h, high))
            else:
                block = pj.at[h, z, pl.ds(far, HALF)]
                moves.append((cov.at[here_rows, column], block, 2, h, jnp.logical_and(low, low_has_far)))
                moves.append(
                    (info.at[here_rows, column], block, 2, h, jnp.logical_and(high, jnp.logical_not(low_has_far)))
                )
        moves.append((st_v.at[h], pj.at[h, z, pl.ds(tail, 8)], 3, h, low))
        moves.append((st_v.at[h], pj.at[h, z, pl.ds(tail + 8, 8)], 4, h, high))
    state_moves = [(trans.at[pl.ds(h * HALF, HALF)], av.at[h, z], 5, h, high) for h in range(2)]

    def shift(source, target, k, h):
        return pltpu.make_async_remote_copy(
            src_ref=source, dst_ref=target, send_sem=shift_send.at[k, h], recv_sem=shift_recv.at[k],
            device_id=(target_base + h, z), device_id_type=MESH,
        )

    def start_moves(chosen):
        for source, target, k, h, active in chosen:
            here = target_base + h == t

            @pl.when(jnp.logical_and(active, here))
            def _():
                pltpu.make_async_copy(source, target, shift_recv.at[k]).start()

            @pl.when(jnp.logical_and(active, jnp.logical_not(here)))
            def _():
                shift(source, target, k, h).start()

    start_moves(moves)
    await_bytes(pj.at[core, z, pl.ds(0, near * HALF)], shift_recv.at[0])
    await_bytes(pj.at[core, z, pl.ds(near * HALF, near * HALF)], shift_recv.at[1])
    await_bytes(pj.at[core, z, pl.ds(far, HALF)], shift_recv.at[2])
    await_bytes(pj.at[core, z, pl.ds(tail, 8)], shift_recv.at[3])
    await_bytes(pj.at[core, z, pl.ds(tail + 8, 8)], shift_recv.at[4])

    def part(kind, h, owner):
        buffer, rows_each = ((pj, (tail + 16) // CHUNKS), (av, HALF // CHUNKS))[kind // CHUNKS]
        return buffer.at[h, owner, pl.ds(kind % CHUNKS * rows_each, rows_each)]

    def parts(kind, h, count):
        buffer, rows_each = ((pj, (tail + 16) // CHUNKS), (av, HALF // CHUNKS))[kind // CHUNKS]
        return buffer.at[h, pl.ds(0, count), pl.ds(kind % CHUNKS * rows_each, rows_each)]

    def copy(kind, owner, way):
        device = ((t, up), (t, down), (partner, z))[way]
        ref = part(kind, core, owner)
        return pltpu.make_async_remote_copy(
            src_ref=ref, dst_ref=ref, send_sem=send.at[kind, way], recv_sem=recv.at[kind, core, owner],
            device_id=device, device_id_type=MESH,
        )

    def arrived(kind, h, owner):
        await_bytes(part(kind, h, owner), recv.at[kind, h, owner])

    def begin(kinds):
        for kind in kinds:
            for way in range(3):
                copy(kind, z, way).start()

    def hop(kinds, step):
        before, after = lax.rem(z - step + Z, Z), lax.rem(z + step, Z)
        for kind in kinds:
            arrived(kind, core, before)

            @pl.when(jnp.logical_or(step < H - 1, core == 0))
            def _():
                copy(kind, before, 0).start()

            arrived(kind, core, after)

            @pl.when(jnp.logical_or(step < H - 1, core == 1))
            def _():
                copy(kind, after, 1).start()

            copy(kind, before, 2).start()
            copy(kind, after, 2).start()

    def last_hop(kinds):
        far = lax.rem(z + H, Z)
        for kind in kinds:
            arrived(kind, core, far)
            copy(kind, far, 2).start()

    def completed(step):
        owner = jnp.where(lax.rem(step + z, 2) == 1, lax.rem(z + step, Z), lax.rem(z - step + Z, Z))
        return owner // 2

    def store(index, row, column, block):
        top, rest = split(block)
        where = (pl.ds(pl.multiple_of(row * LANES, LANES), LANES), pl.ds(pl.multiple_of(column * LANES, LANES), LANES))
        (p_high, j_high)[index][where] = top
        (p_low, j_low)[index][where] = rest

    def unpack(step):
        row = completed(step)
        for owner in (2 * row, 2 * row + 1):
            for kind in matrices:
                arrived(kind, 1 - core, owner)

        def block(k):
            return jnp.concatenate(
                [pj[h, 2 * row + i, k * HALF : (k + 1) * HALF] for i in range(2) for h in range(2)], axis=0
            )

        for index in range(2):
            for k in range(near):
                column = lax.rem(row + k, supers)
                value = block(index * near + k)
                store(index, row, column, value)
                if k:
                    store(index, column, row, value.T)
        column = lax.rem(row + near, supers)
        value = block(2 * near)
        for index in range(2):
            @pl.when((row < near) == (index == 0))
            def _():
                store(index, row, column, value)
                store(index, column, row, value.T)

    matrices, states = tuple(range(CHUNKS)), tuple(range(CHUNKS, 2 * CHUNKS))
    lag = min(LAG, H - 1)
    begin(matrices)
    start_moves(state_moves)

    def first_steps(step, _):
        hop(matrices, step)

        @pl.when(step > 1)
        def _():
            unpack(step - 1)

        return 0

    lax.fori_loop(1, lag + 1, first_steps, 0)
    await_bytes(av.at[core, z], shift_recv.at[5])
    begin(states)

    def later_steps(step, _):
        hop(matrices, step)
        hop(states, step - lag)
        unpack(step - 1)
        return 0

    lax.fori_loop(lag + 1, H, later_steps, 0)
    last_hop(matrices)
    pending = list(range(H - lag, H))

    def next_hop():
        if pending:
            hop(states, pending.pop(0))

    next_hop()
    unpack(H - 1)
    unpack(H)
    pj_save = pltpu.make_async_copy(pj, pj_out, save.at[0])
    pj_save.start()

    width = min(256, size)
    unit = (
        lax.broadcasted_iota(jnp.int32, (width, width), 0) == lax.broadcasted_iota(jnp.int32, (width, width), 1)
    ).astype(F32)
    for q in range(size // width):
        columns = slice(q * width, (q + 1) * width)
        product = dot(p_high[...], j_high[:, columns])
        corner = product[columns]
        inverse = 1.0 / (1.0 + jnp.sum(corner * unit, axis=0, keepdims=True))
        scale[:, columns] = jnp.broadcast_to(inverse, (8, width))
        series[:, columns] = (-product * inverse).astype(BF16)
        series[columns, columns] = (unit - (unit + corner) * inverse).astype(BF16)
    next_hop()
    total = 0.0
    for source, target in ((series, square), (square, fourth)):
        for q in range(size // width):
            columns = slice(q * width, (q + 1) * width)
            product = dot(source[...], source[:, columns])
            target[:, columns] = product.astype(BF16)
            if target is fourth:
                total = total + jnp.sum(product * product)
        next_hop()

    def agree(value, axis, index, peers):
        good[axis, index] = value
        copies = [
            pltpu.make_async_remote_copy(
                src_ref=good.at[axis, index], dst_ref=good.at[axis, index], send_sem=good_send.at[axis, k],
                recv_sem=good_recv.at[axis, index], device_id=(peer, z), device_id_type=MESH,
            )
            for k, peer in enumerate(peers)
        ]
        for one in copies:
            one.start()

        def result():
            count = len(peers) + 1
            for k in range(1, count):
                other = lax.rem(index + k, count)
                await_bytes(good.at[axis, other], good_recv.at[axis, other])
            value = good[axis, 0]
            for k in range(1, count):
                value = jnp.minimum(value, good[axis, k])
            for one in copies:
                one.wait_send()
            return value

        return result

    bounded = jnp.where(total <= LIMIT * LIMIT, 1.0, 0.0).astype(F32)
    fast_result = agree(jnp.broadcast_to(bounded, (8, LANES)), 0, chip_fast, fast_peers)

    inverse = scale[0:1]

    def approximate(value):
        result = value * inverse
        for factor in (series, square, fourth):
            result = result + dot(result.astype(BF16), factor[...])
        return result

    def exact(value, top, rest):
        count = value.shape[0]
        big, small = split(value)
        both = dot(jnp.concatenate([big, small], axis=0), top[...])
        return both[:count] + both[count:] + dot(big, rest[...])

    def vector_row(k):
        at = slice(tail + 8 * k, tail + 8 * k + 8)
        tiles = [
            (pj[0, 2 * s, at] + pj[1, 2 * s, at]) + (pj[0, 2 * s + 1, at] + pj[1, 2 * s + 1, at])
            for s in range(supers)
        ]
        return jnp.concatenate(tiles, axis=1)

    target = av[core, z]
    x = approximate(target)
    stacked = exact(jnp.concatenate([x, vector_row(1)], axis=0), p_high, p_low)
    y = stacked[:HALF]
    combined = vector_row(0) + stacked[HALF:]
    next_hop()
    residual = target - x - exact(y, j_high, j_low)
    change = approximate(residual)
    x = x + change
    moved = exact(change, p_high, p_low)
    y = y + moved
    residual = residual - change - exact(moved, j_high, j_low)
    slow_result = agree(fast_result(), 1, chip_slow, slow_peers)
    while pending:
        next_hop()
    last_hop(states)
    change = approximate(residual)
    x = x + change
    moved = dot(change.astype(BF16), p_high[...])
    y = y + moved
    small[...] = jnp.zeros((8, LANES), F32)
    small[:, 0:HALF] = lax.dot_general(
        combined, x, (((1,), (1,)), ((), ())), precision=HIGHEST, preferred_element_type=F32
    )
    owner_device = jnp.where(low, base_high, base_high + 1)
    mine = owner_device == t

    def give(source, target, arrival, departure):
        @pl.when(mine)
        def _():
            pltpu.make_async_copy(source, target, arrival).start()

        @pl.when(jnp.logical_not(mine))
        def _():
            pltpu.make_async_remote_copy(
                src_ref=source, dst_ref=target, send_sem=departure, recv_sem=arrival,
                device_id=(owner_device, z), device_id_type=MESH,
            ).start()

    give(small, small_in.at[core], back_recv.at[supers, core], back_send.at[1])

    y_high, y_low = split(y)
    y_both = jnp.concatenate([y_high, y_low], axis=0)

    def product_steps(step, _):
        row = completed(step)
        for owner in (2 * row, 2 * row + 1):
            for kind in states:
                arrived(kind, 1 - core, owner)
        block = jnp.concatenate(
            [av[0, 2 * row], av[1, 2 * row], av[0, 2 * row + 1], av[1, 2 * row + 1]], axis=0
        )
        top, rest = split(block)
        both = dot_nt(y_both, top)
        rows[row] = both[:HALF] + both[HALF:] + dot_nt(y_high, rest)
        give(rows.at[row], rows_in.at[core, row], back_recv.at[row, core], back_send.at[0])
        return 0

    lax.fori_loop(1, H + 1, product_steps, 0)
    a_save = pltpu.make_async_copy(av, a_out, save.at[1])
    a_save.start()
    good_out[...] = slow_result()
    fetches[2].wait()

    @pl.when(low)
    def _():
        cov_out[...] = state_cov[...]
        mean_out[...] = vec[0]

    @pl.when(high)
    def _():
        for step in range(1, H + 1):
            row = completed(step)
            column = pl.ds(pl.multiple_of(row * LANES, LANES), LANES)
            for h in range(2):
                await_bytes(rows_in.at[h, row], back_recv.at[row, h])
                cov_out[h * HALF : (h + 1) * HALF, column] = (
                    rows_in[h, row] + state_cov[h * HALF : (h + 1) * HALF, column]
                )
        for h in range(2):
            await_bytes(small_in.at[h], back_recv.at[supers, h])
        mean_out[...] = vec[0] + jnp.concatenate([small_in[0, 0:1, 0:HALF], small_in[1, 0:1, 0:HALF]], axis=1)

    for kind in matrices + states:
        await_bytes(parts(kind, core, Z), send.at[kind, 2])
        for way in range(2):
            @pl.when(core == way)
            def _():
                await_bytes(parts(kind, core, H), send.at[kind, way])

            @pl.when(core != way)
            def _():
                await_bytes(parts(kind, core, H - 1), send.at[kind, way])
    pj_save.wait()
    a_save.wait()
    for h in range(2):
        away = target_base + h != t
        for k, count in ((0, near), (1, near), (2, 1)):
            side = (low, high, low == low_has_far)[k]

            @pl.when(jnp.logical_and(side, away))
            def _():
                await_bytes(pj.at[h, 0, pl.ds(0, count * HALF)], shift_send.at[k, h])

        for k, side in ((3, low), (4, high)):
            @pl.when(jnp.logical_and(side, away))
            def _():
                await_bytes(st_v.at[h], shift_send.at[k, h])

        @pl.when(jnp.logical_and(high, away))
        def _():
            await_bytes(av.at[h, 0], shift_send.at[5, h])

    @pl.when(jnp.logical_not(mine))
    def _():
        await_bytes(rows, back_send.at[0])
        await_bytes(small, back_send.at[1])


def return_kernel(T, rows, small, cov, mean, cov_out, mean_out, rows_in, small_in, recv, send):
    t, z, core, low, base_low, base_high = place(T)
    high = jnp.logical_not(low)
    owner = jnp.where(low, base_high, base_high + 1)
    partner = t + 1 - 2 * core
    opposite = jnp.where(low, base_high, base_low)
    barrier = pltpu.get_barrier_semaphore()
    for device in ((partner, z), (opposite, z), (opposite + 1, z)):
        pl.semaphore_signal(barrier, inc=1, device_id=device, device_id_type=MESH)
    pl.semaphore_wait(barrier, 3)
    moves = ((rows, rows_in.at[core], 0), (small, small_in.at[core], 1))
    here = owner == t

    def back(source, target, k):
        return pltpu.make_async_remote_copy(
            src_ref=source, dst_ref=target, send_sem=send.at[k], recv_sem=recv.at[k, core],
            device_id=(owner, z), device_id_type=MESH,
        )

    for source, target, k in moves:
        @pl.when(here)
        def _():
            pltpu.make_async_copy(source, target, recv.at[k, core]).start()

        @pl.when(jnp.logical_not(here))
        def _():
            back(source, target, k).start()

    @pl.when(low)
    def _():
        cov_out[...] = cov[...]
        mean_out[...] = mean[...]

    @pl.when(high)
    def _():
        for h in range(2):
            await_bytes(rows_in.at[h], recv.at[0, h])
            cov_out[h * HALF : (h + 1) * HALF] = rows_in[h] + cov[h * HALF : (h + 1) * HALF]
            await_bytes(small_in.at[h], recv.at[1, h])
        mean_out[...] = mean[...] + jnp.concatenate([small_in[0, 0:1, 0:HALF], small_in[1, 0:1, 0:HALF]], axis=1)

    for source, target, k in moves:
        @pl.when(jnp.logical_not(here))
        def _():
            back(source, target, k).wait_send()


def by_factors(operands):
    pj, av = operands
    Z = av.shape[1]
    supers = Z // 2
    near = supers // 2
    size = Z * ROWS
    core = lax.rem(lax.axis_index("tm"), 2)
    z = lax.axis_index("panel")
    blocks = 2 * near + 1
    packed = pj[:, :, : blocks * HALF].reshape(2, supers, 2, blocks, HALF, LANES)
    packed = packed.transpose(1, 3, 2, 0, 4, 5).reshape(supers, blocks, LANES, LANES)

    def whole(index):
        grid = [[None] * supers for _ in range(supers)]
        for row in range(supers):
            for k in range(near + 1):
                if k == near and (row < near) != (index == 0):
                    continue
                block = packed[row, 2 * near if k == near else index * near + k]
                column = (row + k) % supers
                grid[row][column] = block
                if k:
                    grid[column][row] = block.T
        return jnp.concatenate([jnp.concatenate(row, axis=1) for row in grid], axis=0)

    cov, info = whole(0), whole(1)
    rows = av.transpose(1, 0, 2, 3).reshape(size, size)
    tiles = pj[:, :, blocks * HALF :: 8].sum(axis=0).reshape(supers, 2, 2, LANES).sum(axis=1)
    mean, infovec = tiles[:, 0].reshape(size), tiles[:, 1].reshape(size)
    mm = functools.partial(jnp.dot, precision=HIGHEST)
    lower_factor = jnp.linalg.cholesky(cov)
    inner = jnp.eye(size, dtype=F32) + mm(lower_factor.T, mm(info, lower_factor))
    inner_factor = jnp.linalg.cholesky(inner)
    mixed = mm(rows, lower_factor)
    factor = jax.scipy.linalg.solve_triangular(inner_factor, mixed.T, lower=True).T
    mine = lax.dynamic_slice_in_dim(factor, z * ROWS + core * HALF, HALF, 0)
    mixed_mine = lax.dynamic_slice_in_dim(mixed, z * ROWS + core * HALF, HALF, 0)
    right = jax.scipy.linalg.solve_triangular(lower_factor, mean, lower=True) + mm(infovec, lower_factor)
    weight = jax.scipy.linalg.cho_solve((inner_factor, True), right)
    small = jnp.zeros((8, LANES), F32).at[:, 0:HALF].set(mm(mixed_mine, weight)[None])
    return mm(mine, factor.T), small


def solution(mesh):
    T, Z = mesh.shape["tm"], mesh.shape["panel"]
    near = Z // 4
    size = Z * ROWS
    vmem = pl.BlockSpec(memory_space=pltpu.VMEM)
    hbm = pl.BlockSpec(memory_space=pltpu.HBM)
    dma = pltpu.SemaphoreType.DMA
    supers = Z // 2
    pj_shape = (2, Z, (2 * near + 1) * HALF + 16, LANES)
    a_shape = (2, Z, HALF, size)
    struct = lambda *shape: jax.ShapeDtypeStruct(shape, F32)
    scratch = lambda *shape: pltpu.VMEM(shape, F32)

    def body(*arrays):
        elem_trans, elem_cov, elem_info, elem_mean, elem_infovec = arrays
        new_cov, new_mean, good, pj, av = pl.pallas_call(
            functools.partial(solve_kernel, T, Z),
            name="gather_and_solve",
            out_shape=(
                struct(ROWS, size), struct(1, ROWS), struct(8, LANES), struct(*pj_shape), struct(*a_shape)
            ),
            in_specs=[hbm] * 5,
            out_specs=(vmem, vmem, vmem, hbm, hbm),
            scratch_shapes=[
                scratch(*pj_shape),
                scratch(*a_shape),
                scratch(2, 1, ROWS),
                scratch(2, 8, LANES),
                scratch(ROWS, size),
                scratch(2, supers, HALF, LANES),
                scratch(2, 8, LANES),
                scratch(supers, HALF, LANES),
                scratch(8, LANES),
                scratch(2, 4, 8, LANES),
            ]
            + [pltpu.VMEM((size, size), BF16)] * 7
            + [
                scratch(8, size),
                dma((2 * CHUNKS, 2, Z)),
                dma((2 * CHUNKS, 3)),
                dma((6,)),
                dma((6, 2)),
                dma((3,)),
                dma((supers + 1, 2)),
                dma((2,)),
                dma((2, 4)),
                dma((2, 4)),
                dma((2,)),
            ],
            compiler_params=pltpu.CompilerParams(
                collective_id=0, has_side_effects=True, vmem_limit_bytes=60 * 2**20
            ),
        )(elem_trans[0], elem_cov[0], elem_info[0], elem_mean, elem_infovec)
        def otherwise(operands):
            return pl.pallas_call(
                functools.partial(return_kernel, T),
                name="rows_to_owner",
                out_shape=(struct(ROWS, size), struct(1, ROWS)),
                in_specs=[vmem] * 4,
                out_specs=(vmem, vmem),
                scratch_shapes=[scratch(2, HALF, size), scratch(2, 8, LANES), dma((2, 2)), dma((2,))],
                compiler_params=pltpu.CompilerParams(
                    collective_id=1, has_side_effects=True, vmem_limit_bytes=16 * 2**20
                ),
            )(*by_factors(operands[:2]), operands[2], operands[3])

        new_cov, new_mean = lax.cond(
            good[0, 0] > 0.5, lambda *_: (new_cov, new_mean), lambda *operands: otherwise(operands),
            pj, av, elem_cov[0], elem_mean,
        )
        return new_cov[None], new_mean

    matrix, line = P("tm", "panel", None), P("tm", "panel")
    return jax.shard_map(
        body,
        mesh=mesh,
        in_specs=(matrix, matrix, matrix, line, line),
        out_specs=(matrix, line),
        check_vma=False,
    )
```

```python
import functools

import jax
import jax.numpy as jnp
from jax import lax
from jax.experimental import pallas as pl
from jax.experimental.pallas import tpu as pltpu
from jax.sharding import PartitionSpec as P

MESH = pl.DeviceIdType.MESH
HIGHEST = lax.Precision.HIGHEST
F32 = jnp.float32
BF16 = jnp.bfloat16
ROWS = 64
HALF = 32
LANES = 128
LAG = 2
CHUNKS = 2
LIMIT = 0.16


def split(value):
    high = value.astype(BF16)
    return high, (value - high.astype(F32)).astype(BF16)


def dot(left, right):
    return jnp.dot(left, right, preferred_element_type=F32)


def dot_nt(left, right):
    return lax.dot_general(left, right, (((1,), (1,)), ((), ())), preferred_element_type=F32)


def place(T):
    t = lax.axis_index("tm")
    z = lax.axis_index("panel")
    distance = T // 2
    core = lax.rem(t, 2)
    low = t < distance
    base_low = lax.rem(t, distance) - core
    base_high = base_low + distance
    return t, z, core, low, base_low, base_high


def await_bytes(ref, sem):
    pltpu.make_async_copy(ref, ref, sem).wait()


def solve_kernel(
    T, Z,
    trans, cov, info, mean, infovec,
    cov_out, mean_out, good_out, pj_out, a_out,
    pj, av, vec, st_v, state_cov, rows_in, small_in, rows, small, good,
    p_high, p_low, j_high, j_low, series, square, fourth, scale,
    recv, send, shift_recv, shift_send, local, back_recv, back_send, good_recv, good_send, save,
):
    t, z, core, low, base_low, base_high = place(T)
    supers = Z // 2
    near = supers // 2
    H = Z // 2
    size = Z * ROWS
    partner = t + 1 - 2 * core
    opposite = jnp.where(low, base_high, base_low)
    up, down = lax.rem(z + 1, Z), lax.rem(z + Z - 1, Z)

    fast = min(4, T // 2)
    slow = T // 2 // fast
    chip = t // 2
    chip_slow, chip_fast = chip // fast, lax.rem(chip, fast)
    fast_peers = [(chip_slow * fast + lax.rem(chip_fast + k, fast)) * 2 + core for k in range(1, fast)]
    slow_peers = [(lax.rem(chip_slow + k, slow) * fast + chip_fast) * 2 + core for k in range(1, slow)]
    devices = [(t, up), (t, down), (partner, z), (opposite, z), (opposite + 1, z)]
    devices += [(peer, z) for peer in fast_peers + slow_peers]
    barrier = pltpu.get_barrier_semaphore()
    for device in devices:
        pl.semaphore_signal(barrier, inc=1, device_id=device, device_id_type=MESH)

    fetches = [
        pltpu.make_async_copy(source, target, local.at[k])
        for k, (source, target) in enumerate(((mean, vec.at[0]), (infovec, vec.at[1]), (cov, state_cov)))
    ]
    for fetch in fetches:
        fetch.start()
    fetches[0].wait()
    fetches[1].wait()
    vector = jnp.where(low, vec[0], vec[1])
    nothing = jnp.zeros_like(vector)
    vector = jnp.where(
        lax.rem(z, 2) == 0,
        jnp.concatenate([vector, nothing], axis=1),
        jnp.concatenate([nothing, vector], axis=1),
    )
    lane = lax.broadcasted_iota(jnp.int32, (8, LANES), 1)
    for h in range(2):
        start = lax.rem(z, 2) * ROWS + h * HALF
        mine = jnp.logical_and(lane >= start, lane < start + HALF)
        st_v[h] = jnp.where(mine, jnp.broadcast_to(vector, (8, LANES)), 0.0)
    own_super = z // 2
    pl.semaphore_wait(barrier, len(devices))

    target_base = jnp.where(core == 0, base_low, base_high)
    high = jnp.logical_not(low)
    low_has_far = own_super < near
    far = 2 * near * HALF
    tail = far + HALF
    moves = []
    for h in range(2):
        here_rows = pl.ds(h * HALF, HALF)
        for k in range(near + 1):
            column = pl.ds(pl.multiple_of(lax.rem(own_super + k, supers) * LANES, LANES), LANES)
            if k < near:
                moves.append((cov.at[here_rows, column], pj.at[h, z, pl.ds(k * HALF, HALF)], 0, h, low))
                moves.append((info.at[here_rows, column], pj.at[h, z, pl.ds((near + k) * HALF, HALF)], 1, h, high))
            else:
                block = pj.at[h, z, pl.ds(far, HALF)]
                moves.append((cov.at[here_rows, column], block, 2, h, jnp.logical_and(low, low_has_far)))
                moves.append(
                    (info.at[here_rows, column], block, 2, h, jnp.logical_and(high, jnp.logical_not(low_has_far)))
                )
        moves.append((st_v.at[h], pj.at[h, z, pl.ds(tail, 8)], 3, h, low))
        moves.append((st_v.at[h], pj.at[h, z, pl.ds(tail + 8, 8)], 4, h, high))
    state_moves = [(trans.at[pl.ds(h * HALF, HALF)], av.at[h, z], 5, h, high) for h in range(2)]

    def shift(source, target, k, h):
        return pltpu.make_async_remote_copy(
            src_ref=source, dst_ref=target, send_sem=shift_send.at[k, h], recv_sem=shift_recv.at[k],
            device_id=(target_base + h, z), device_id_type=MESH,
        )

    def start_moves(chosen):
        for source, target, k, h, active in chosen:
            here = target_base + h == t

            @pl.when(jnp.logical_and(active, here))
            def _():
                pltpu.make_async_copy(source, target, shift_recv.at[k]).start()

            @pl.when(jnp.logical_and(active, jnp.logical_not(here)))
            def _():
                shift(source, target, k, h).start()

    start_moves(moves)
    await_bytes(pj.at[core, z, pl.ds(0, near * HALF)], shift_recv.at[0])
    await_bytes(pj.at[core, z, pl.ds(near * HALF, near * HALF)], shift_recv.at[1])
    await_bytes(pj.at[core, z, pl.ds(far, HALF)], shift_recv.at[2])
    await_bytes(pj.at[core, z, pl.ds(tail, 8)], shift_recv.at[3])
    await_bytes(pj.at[core, z, pl.ds(tail + 8, 8)], shift_recv.at[4])

    def part(kind, h, owner):
        buffer, rows_each = ((pj, (tail + 16) // CHUNKS), (av, HALF // CHUNKS))[kind // CHUNKS]
        return buffer.at[h, owner, pl.ds(kind % CHUNKS * rows_each, rows_each)]

    def parts(kind, h, count):
        buffer, rows_each = ((pj, (tail + 16) // CHUNKS), (av, HALF // CHUNKS))[kind // CHUNKS]
        return buffer.at[h, pl.ds(0, count), pl.ds(kind % CHUNKS * rows_each, rows_each)]

    def copy(kind, owner, way):
        device = ((t, up), (t, down), (partner, z))[way]
        ref = part(kind, core, owner)
        return pltpu.make_async_remote_copy(
            src_ref=ref, dst_ref=ref, send_sem=send.at[kind, way], recv_sem=recv.at[kind, core, owner],
            device_id=device, device_id_type=MESH,
        )

    def arrived(kind, h, owner):
        await_bytes(part(kind, h, owner), recv.at[kind, h, owner])

    def begin(kinds):
        for kind in kinds:
            for way in range(3):
                copy(kind, z, way).start()

    def hop(kinds, step):
        before, after = lax.rem(z - step + Z, Z), lax.rem(z + step, Z)
        for kind in kinds:
            arrived(kind, core, before)

            @pl.when(jnp.logical_or(step < H - 1, core == 0))
            def _():
                copy(kind, before, 0).start()

            arrived(kind, core, after)

            @pl.when(jnp.logical_or(step < H - 1, core == 1))
            def _():
                copy(kind, after, 1).start()

            copy(kind, before, 2).start()
            copy(kind, after, 2).start()

    def last_hop(kinds):
        far = lax.rem(z + H, Z)
        for kind in kinds:
            arrived(kind, core, far)
            copy(kind, far, 2).start()

    def completed(step):
        owner = jnp.where(lax.rem(step + z, 2) == 1, lax.rem(z + step, Z), lax.rem(z - step + Z, Z))
        return owner // 2

    def store(index, row, column, block):
        top, rest = split(block)
        where = (pl.ds(pl.multiple_of(row * LANES, LANES), LANES), pl.ds(pl.multiple_of(column * LANES, LANES), LANES))
        (p_high, j_high)[index][where] = top
        (p_low, j_low)[index][where] = rest

    def unpack(step):
        row = completed(step)
        for owner in (2 * row, 2 * row + 1):
            for kind in matrices:
                arrived(kind, 1 - core, owner)

        def block(k):
            return jnp.concatenate(
                [pj[h, 2 * row + i, k * HALF : (k + 1) * HALF] for i in range(2) for h in range(2)], axis=0
            )

        for index in range(2):
            for k in range(near):
                column = lax.rem(row + k, supers)
                value = block(index * near + k)
                store(index, row, column, value)
                if k:
                    store(index, column, row, value.T)
        column = lax.rem(row + near, supers)
        value = block(2 * near)
        for index in range(2):
            @pl.when((row < near) == (index == 0))
            def _():
                store(index, row, column, value)
                store(index, column, row, value.T)

    matrices, states = tuple(range(CHUNKS)), tuple(range(CHUNKS, 2 * CHUNKS))
    lag = min(LAG, H - 1)
    begin(matrices)
    start_moves(state_moves)

    def first_steps(step, _):
        hop(matrices, step)

        @pl.when(step > 1)
        def _():
            unpack(step - 1)

        return 0

    lax.fori_loop(1, lag + 1, first_steps, 0)
    await_bytes(av.at[core, z], shift_recv.at[5])
    begin(states)

    def later_steps(step, _):
        hop(matrices, step)
        hop(states, step - lag)
        unpack(step - 1)
        return 0

    lax.fori_loop(lag + 1, H, later_steps, 0)
    last_hop(matrices)
    pending = list(range(H - lag, H))

    def next_hop():
        if pending:
            hop(states, pending.pop(0))

    next_hop()
    unpack(H - 1)
    unpack(H)
    pj_save = pltpu.make_async_copy(pj, pj_out, save.at[0])
    pj_save.start()

    width = min(256, size)
    unit = (
        lax.broadcasted_iota(jnp.int32, (width, width), 0) == lax.broadcasted_iota(jnp.int32, (width, width), 1)
    ).astype(F32)
    for q in range(size // width):
        columns = slice(q * width, (q + 1) * width)
        product = dot(p_high[...], j_high[:, columns])
        corner = product[columns]
        inverse = 1.0 / (1.0 + jnp.sum(corner * unit, axis=0, keepdims=True))
        scale[:, columns] = jnp.broadcast_to(inverse, (8, width))
        series[:, columns] = (-product * inverse).astype(BF16)
        series[columns, columns] = (unit - (unit + corner) * inverse).astype(BF16)
    next_hop()
    total = 0.0
    for source, target in ((series, square), (square, fourth)):
        for q in range(size // width):
            columns = slice(q * width, (q + 1) * width)
            product = dot(source[...], source[:, columns])
            target[:, columns] = product.astype(BF16)
            if target is fourth:
                total = total + jnp.sum(product * product)
        next_hop()

    def agree(value, axis, index, peers):
        good[axis, index] = value
        copies = [
            pltpu.make_async_remote_copy(
                src_ref=good.at[axis, index], dst_ref=good.at[axis, index], send_sem=good_send.at[axis, k],
                recv_sem=good_recv.at[axis, index], device_id=(peer, z), device_id_type=MESH,
            )
            for k, peer in enumerate(peers)
        ]
        for one in copies:
            one.start()

        def result():
            count = len(peers) + 1
            for k in range(1, count):
                other = lax.rem(index + k, count)
                await_bytes(good.at[axis, other], good_recv.at[axis, other])
            value = good[axis, 0]
            for k in range(1, count):
                value = jnp.minimum(value, good[axis, k])
            for one in copies:
                one.wait_send()
            return value

        return result

    bounded = jnp.where(total <= LIMIT * LIMIT, 1.0, 0.0).astype(F32)
    fast_result = agree(jnp.broadcast_to(bounded, (8, LANES)), 0, chip_fast, fast_peers)

    inverse = scale[0:1]

    def approximate(value):
        result = value * inverse
        for factor in (series, square, fourth):
            result = result + dot(result.astype(BF16), factor[...])
        return result

    def exact(value, top, rest):
        count = value.shape[0]
        big, small = split(value)
        both = dot(jnp.concatenate([big, small], axis=0), top[...])
        return both[:count] + both[count:] + dot(big, rest[...])

    def vector_row(k):
        at = slice(tail + 8 * k, tail + 8 * k + 8)
        tiles = [
            (pj[0, 2 * s, at] + pj[1, 2 * s, at]) + (pj[0, 2 * s + 1, at] + pj[1, 2 * s + 1, at])
            for s in range(supers)
        ]
        return jnp.concatenate(tiles, axis=1)

    target = av[core, z]
    x = approximate(target)
    stacked = exact(jnp.concatenate([x, vector_row(1)], axis=0), p_high, p_low)
    y = stacked[:HALF]
    combined = vector_row(0) + stacked[HALF:]
    next_hop()
    residual = target - x - exact(y, j_high, j_low)
    change = approximate(residual)
    x = x + change
    moved = dot(change.astype(BF16), p_high[...])
    y = y + moved
    residual = residual - change - dot(moved.astype(BF16), j_high[...])
    slow_result = agree(fast_result(), 1, chip_slow, slow_peers)
    while pending:
        next_hop()
    last_hop(states)
    change = approximate(residual)
    x = x + change
    moved = dot(change.astype(BF16), p_high[...])
    y = y + moved
    small[...] = jnp.zeros((8, LANES), F32)
    small[:, 0:HALF] = lax.dot_general(
        combined, x, (((1,), (1,)), ((), ())), precision=HIGHEST, preferred_element_type=F32
    )
    owner_device = jnp.where(low, base_high, base_high + 1)
    mine = owner_device == t

    def give(source, target, arrival, departure):
        @pl.when(mine)
        def _():
            pltpu.make_async_copy(source, target, arrival).start()

        @pl.when(jnp.logical_not(mine))
        def _():
            pltpu.make_async_remote_copy(
                src_ref=source, dst_ref=target, send_sem=departure, recv_sem=arrival,
                device_id=(owner_device, z), device_id_type=MESH,
            ).start()

    give(small, small_in.at[core], back_recv.at[supers, core], back_send.at[1])

    y_high, y_low = split(y)
    y_both = jnp.concatenate([y_high, y_low], axis=0)

    def product_steps(step, _):
        row = completed(step)
        for owner in (2 * row, 2 * row + 1):
            for kind in states:
                arrived(kind, 1 - core, owner)
        block = jnp.concatenate(
            [av[0, 2 * row], av[1, 2 * row], av[0, 2 * row + 1], av[1, 2 * row + 1]], axis=0
        )
        top, rest = split(block)
        both = dot_nt(y_both, top)
        rows[row] = both[:HALF] + both[HALF:] + dot_nt(y_high, rest)
        give(rows.at[row], rows_in.at[core, row], back_recv.at[row, core], back_send.at[0])
        return 0

    lax.fori_loop(1, H + 1, product_steps, 0)
    a_save = pltpu.make_async_copy(av, a_out, save.at[1])
    a_save.start()
    good_out[0] = jnp.min(slow_result())
    fetches[2].wait()

    @pl.when(low)
    def _():
        cov_out[...] = state_cov[...]
        mean_out[...] = vec[0]

    @pl.when(high)
    def _():
        for step in range(1, H + 1):
            row = completed(step)
            column = pl.ds(pl.multiple_of(row * LANES, LANES), LANES)
            for h in range(2):
                await_bytes(rows_in.at[h, row], back_recv.at[row, h])
                cov_out[h * HALF : (h + 1) * HALF, column] = (
                    rows_in[h, row] + state_cov[h * HALF : (h + 1) * HALF, column]
                )
        for h in range(2):
            await_bytes(small_in.at[h], back_recv.at[supers, h])
        mean_out[...] = vec[0] + jnp.concatenate([small_in[0, 0:1, 0:HALF], small_in[1, 0:1, 0:HALF]], axis=1)

    for kind in matrices + states:
        await_bytes(parts(kind, core, Z), send.at[kind, 2])
        for way in range(2):
            @pl.when(core == way)
            def _():
                await_bytes(parts(kind, core, H), send.at[kind, way])

            @pl.when(core != way)
            def _():
                await_bytes(parts(kind, core, H - 1), send.at[kind, way])
    pj_save.wait()
    a_save.wait()
    for h in range(2):
        away = target_base + h != t
        for k, count in ((0, near), (1, near), (2, 1)):
            side = (low, high, low == low_has_far)[k]

            @pl.when(jnp.logical_and(side, away))
            def _():
                await_bytes(pj.at[h, 0, pl.ds(0, count * HALF)], shift_send.at[k, h])

        for k, side in ((3, low), (4, high)):
            @pl.when(jnp.logical_and(side, away))
            def _():
                await_bytes(st_v.at[h], shift_send.at[k, h])

        @pl.when(jnp.logical_and(high, away))
        def _():
            await_bytes(av.at[h, 0], shift_send.at[5, h])

    @pl.when(jnp.logical_not(mine))
    def _():
        await_bytes(rows, back_send.at[0])
        await_bytes(small, back_send.at[1])


def return_kernel(T, rows, small, cov, mean, cov_out, mean_out, rows_in, small_in, recv, send):
    t, z, core, low, base_low, base_high = place(T)
    high = jnp.logical_not(low)
    owner = jnp.where(low, base_high, base_high + 1)
    partner = t + 1 - 2 * core
    opposite = jnp.where(low, base_high, base_low)
    barrier = pltpu.get_barrier_semaphore()
    for device in ((partner, z), (opposite, z), (opposite + 1, z)):
        pl.semaphore_signal(barrier, inc=1, device_id=device, device_id_type=MESH)
    pl.semaphore_wait(barrier, 3)
    moves = ((rows, rows_in.at[core], 0), (small, small_in.at[core], 1))
    here = owner == t

    def back(source, target, k):
        return pltpu.make_async_remote_copy(
            src_ref=source, dst_ref=target, send_sem=send.at[k], recv_sem=recv.at[k, core],
            device_id=(owner, z), device_id_type=MESH,
        )

    for source, target, k in moves:
        @pl.when(here)
        def _():
            pltpu.make_async_copy(source, target, recv.at[k, core]).start()

        @pl.when(jnp.logical_not(here))
        def _():
            back(source, target, k).start()

    @pl.when(low)
    def _():
        cov_out[...] = cov[...]
        mean_out[...] = mean[...]

    @pl.when(high)
    def _():
        for h in range(2):
            await_bytes(rows_in.at[h], recv.at[0, h])
            cov_out[h * HALF : (h + 1) * HALF] = rows_in[h] + cov[h * HALF : (h + 1) * HALF]
            await_bytes(small_in.at[h], recv.at[1, h])
        mean_out[...] = mean[...] + jnp.concatenate([small_in[0, 0:1, 0:HALF], small_in[1, 0:1, 0:HALF]], axis=1)

    for source, target, k in moves:
        @pl.when(jnp.logical_not(here))
        def _():
            back(source, target, k).wait_send()


def by_factors(operands):
    pj, av = operands
    Z = av.shape[1]
    supers = Z // 2
    near = supers // 2
    size = Z * ROWS
    core = lax.rem(lax.axis_index("tm"), 2)
    z = lax.axis_index("panel")
    blocks = 2 * near + 1
    packed = pj[:, :, : blocks * HALF].reshape(2, supers, 2, blocks, HALF, LANES)
    packed = packed.transpose(1, 3, 2, 0, 4, 5).reshape(supers, blocks, LANES, LANES)

    def whole(index):
        grid = [[None] * supers for _ in range(supers)]
        for row in range(supers):
            for k in range(near + 1):
                if k == near and (row < near) != (index == 0):
                    continue
                block = packed[row, 2 * near if k == near else index * near + k]
                column = (row + k) % supers
                grid[row][column] = block
                if k:
                    grid[column][row] = block.T
        return jnp.concatenate([jnp.concatenate(row, axis=1) for row in grid], axis=0)

    cov, info = whole(0), whole(1)
    rows = av.transpose(1, 0, 2, 3).reshape(size, size)
    tiles = pj[:, :, blocks * HALF :: 8].sum(axis=0).reshape(supers, 2, 2, LANES).sum(axis=1)
    mean, infovec = tiles[:, 0].reshape(size), tiles[:, 1].reshape(size)
    mm = functools.partial(jnp.dot, precision=HIGHEST)
    lower_factor = jnp.linalg.cholesky(cov)
    inner = jnp.eye(size, dtype=F32) + mm(lower_factor.T, mm(info, lower_factor))
    inner_factor = jnp.linalg.cholesky(inner)
    mixed = mm(rows, lower_factor)
    factor = jax.scipy.linalg.solve_triangular(inner_factor, mixed.T, lower=True).T
    mine = lax.dynamic_slice_in_dim(factor, z * ROWS + core * HALF, HALF, 0)
    mixed_mine = lax.dynamic_slice_in_dim(mixed, z * ROWS + core * HALF, HALF, 0)
    right = jax.scipy.linalg.solve_triangular(lower_factor, mean, lower=True) + mm(infovec, lower_factor)
    weight = jax.scipy.linalg.cho_solve((inner_factor, True), right)
    small = jnp.zeros((8, LANES), F32).at[:, 0:HALF].set(mm(mixed_mine, weight)[None])
    return mm(mine, factor.T), small


def solution(mesh):
    T, Z = mesh.shape["tm"], mesh.shape["panel"]
    near = Z // 4
    size = Z * ROWS
    vmem = pl.BlockSpec(memory_space=pltpu.VMEM)
    hbm = pl.BlockSpec(memory_space=pltpu.HBM)
    dma = pltpu.SemaphoreType.DMA
    supers = Z // 2
    pj_shape = (2, Z, (2 * near + 1) * HALF + 16, LANES)
    a_shape = (2, Z, HALF, size)
    struct = lambda *shape: jax.ShapeDtypeStruct(shape, F32)
    scratch = lambda *shape: pltpu.VMEM(shape, F32)

    def body(*arrays):
        elem_trans, elem_cov, elem_info, elem_mean, elem_infovec = arrays
        new_cov, new_mean, good, pj, av = pl.pallas_call(
            functools.partial(solve_kernel, T, Z),
            name="gather_and_solve",
            out_shape=(
                struct(ROWS, size), struct(1, ROWS), struct(1), struct(*pj_shape), struct(*a_shape)
            ),
            in_specs=[hbm] * 5,
            out_specs=(vmem, vmem, pl.BlockSpec(memory_space=pltpu.SMEM), hbm, hbm),
            scratch_shapes=[
                scratch(*pj_shape),
                scratch(*a_shape),
                scratch(2, 1, ROWS),
                scratch(2, 8, LANES),
                scratch(ROWS, size),
                scratch(2, supers, HALF, LANES),
                scratch(2, 8, LANES),
                scratch(supers, HALF, LANES),
                scratch(8, LANES),
                scratch(2, 4, 8, LANES),
            ]
            + [pltpu.VMEM((size, size), BF16)] * 7
            + [
                scratch(8, size),
                dma((2 * CHUNKS, 2, Z)),
                dma((2 * CHUNKS, 3)),
                dma((6,)),
                dma((6, 2)),
                dma((3,)),
                dma((supers + 1, 2)),
                dma((2,)),
                dma((2, 4)),
                dma((2, 4)),
                dma((2,)),
            ],
            compiler_params=pltpu.CompilerParams(
                collective_id=0, has_side_effects=True, vmem_limit_bytes=60 * 2**20
            ),
        )(elem_trans[0], elem_cov[0], elem_info[0], elem_mean, elem_infovec)
        def otherwise(operands):
            return pl.pallas_call(
                functools.partial(return_kernel, T),
                name="rows_to_owner",
                out_shape=(struct(ROWS, size), struct(1, ROWS)),
                in_specs=[vmem] * 4,
                out_specs=(vmem, vmem),
                scratch_shapes=[scratch(2, HALF, size), scratch(2, 8, LANES), dma((2, 2)), dma((2,))],
                compiler_params=pltpu.CompilerParams(
                    collective_id=1, has_side_effects=True, vmem_limit_bytes=16 * 2**20
                ),
            )(*by_factors(operands[:2]), operands[2], operands[3])

        new_cov, new_mean = lax.cond(
            good[0] > 0.5, lambda *_: (new_cov, new_mean), lambda *operands: otherwise(operands),
            pj, av, elem_cov[0], elem_mean,
        )
        return new_cov[None], new_mean

    matrix, line = P("tm", "panel", None), P("tm", "panel")
    return jax.shard_map(
        body,
        mesh=mesh,
        in_specs=(matrix, matrix, matrix, line, line),
        out_specs=(matrix, line),
        check_vma=False,
    )
```
